32 devices in a mesh: rad: 4 (over x, core), sec: 8 (over z, y).
Axes of the slice: x: 2, y: 2, z: 4, core: 2. Of those that a mesh axis runs over, the one named last changes fastest.
Arguments:
- gas_fields: float32 [5, 128, 16, 2048], P(None, 'rad', None, 'sec'), may hold values from -8 to 8, as said below
- orbit_shift: int32 [128], P('rad'), may hold values from 0 to 2047
- particle_velocity: float32 [3, 131072], P(None, ('rad', 'sec')), may hold values from -6 to 6
- particle_mass: float32 [131072], P(('rad', 'sec')), may hold values from 0.2 to 2
- particle_stop: float32 [131072], P(('rad', 'sec')), may hold values from 0.1 to 10
- particle_cell: int32 [131072], P(('rad', 'sec')), may hold values from 0 to 131071
- particle_dest: int32 [131072, 1], P(('rad', 'sec')), may hold values from 0 to 31; in each aligned block of 4096 rows (0 to 4095, 4096 to 8191, ...) at most 256 rows name the same one
Outputs:
- gas_next: float32 [5, 128, 16, 2048], P(None, 'rad', None, 'sec')
- arrived_velocity: float32 [3, 262144], P(None, ('rad', 'sec'))
The draws below stay inside these ranges and needn't reach their ends.
Inputs may be any that keep to these rules, and one draw needn't show every extreme that they name: `gas_fields`: field 0 (density) lies between 0.25 and 4 and momentum over density between -2 and 2. `particle_dest`: among the 4096 particles of one device at most 256 name the same destination; in every draw some device sends exactly 256 to one destination.
All inputs are finite; a program needn't handle non-finite values.
Results may differ from the reference program's by a relative error of at most 0.0003.
Values sent between devices are 32-bit elements; how exact they have to be, the bound alone decides.
A program may use at most 128 MiB of HBM per device.

```python
import math
import jax
import jax.numpy as jnp
import numpy as np
from jax import lax

CR = 32
ZL = 16
CP = 256
PD = 4096
NR = 128
NPHI = 2048
CAP = 256
NPART = 131072
N_SEC = 8
DEVICES = 32


def draw_gas_fields(key, part):
    subkeys = jax.random.split(key, 3)
    grid_shape = (1, NR, ZL, NPHI)
    motion_shape = (3, NR, ZL, NPHI)
    density = jnp.exp(jax.random.uniform(subkeys[0], grid_shape, jnp.float32, -0.7, 0.7))
    motion = jnp.clip(0.5 * jax.random.normal(subkeys[1], motion_shape, jnp.float32), -2.0, 2.0) * density
    energy = jnp.exp(jax.random.uniform(subkeys[2], grid_shape, jnp.float32, 0.0, 1.1))
    return jnp.concatenate([density, motion, energy], axis=0)


def place_ends(result, stream_key, low, top_value):
    shape = result.shape
    index_at = [jax.random.randint(jax.random.fold_in(stream_key, axis), (), 0, shape[axis]) for axis in range(len(shape))]
    result = result.at[tuple(index_at)].set(low)
    longest = shape.index(max(shape))
    index_at[longest] = (index_at[longest] + 1) % shape[longest]
    return result.at[tuple(index_at)].set(top_value)


def level_of(stream_key, shape, cuts, least, largest):
    factor_of = 1.0
    for position, blocks in cuts:
        heights = jax.random.uniform(jax.random.fold_in(jax.random.fold_in(stream_key, 6), position), (blocks,), jnp.float32, least / len(cuts), largest / len(cuts))
        factor_of = factor_of * jnp.repeat(jnp.exp(heights), shape[position] // blocks).reshape((-1,) + (1,) * (len(shape) - 1 - position))
    return factor_of


def routed_block(own_key, own, number, rows, number_of, top, most, slope):
    sequence = jax.random.permutation(own_key, number_of)
    crowded, ordinary = shares(number_of, rows * top, most, slope, True), shares(number_of, rows * top, most, slope, False)
    places = jnp.arange(number_of)

    def named(tallies, rotation):
        used = int((tallies > 0).sum())
        fixed = max(1, used // 4)
        moved = fixed + (places - fixed + rotation * (used - fixed)) % max(1, number_of - fixed)
        return jnp.zeros((number_of,), jnp.int32).at[sequence[jnp.where(places < fixed, places, moved)]].set(jnp.asarray(tallies, jnp.int32))

    tallies = jnp.where(number % 4 == 0, named(crowded, number // 4), named(ordinary, number - number // 4 - 1))
    mixed = jax.random.permutation(jax.random.fold_in(own, 3), number_of)
    donor, sink = mixed[0:number_of // 2 * 2:2], mixed[1:number_of // 2 * 2:2]
    margin = jnp.minimum(tallies[donor] - 1, most - tallies[sink]) // 2
    margin = jnp.where((donor == sequence[0]) | (sink == sequence[0]) | (tallies[sink] == 0), 0, jnp.maximum(margin, 0))
    moved = jax.random.randint(jax.random.fold_in(own, 4), (number_of // 2,), 0, 1 << 20) % (margin + 1)
    tallies = tallies.at[donor].add(-moved).at[sink].add(moved)
    items = jnp.searchsorted(jnp.cumsum(tallies), jnp.arange(rows * top), side="right").astype(jnp.int32)
    table = items.reshape(top, rows).T
    table = table[jax.random.permutation(jax.random.fold_in(own, 1), rows)]
    rotation = jax.random.randint(jax.random.fold_in(own, 2), (rows, 1), 0, top)
    return jnp.take_along_axis(table, (jnp.arange(top)[None, :] + rotation) % top, axis=1)


def shares(amount, total, bound, slope, full):
    weights = [(1 << 20) // math.isqrt(standing ** slope) + 1 for standing in range(1, amount + 1)]
    largest = bound if full else min(bound, max(-(-total // amount), total * weights[0] // sum(weights)))
    least = 1 if total - largest >= amount - 1 else 0
    holding, rest = [largest] + [least] * (amount - 1), total - largest - least * (amount - 1)
    while rest > 0:
        candidates = [i for i in range(1, amount) if holding[i] < largest] or [i for i in range(1, amount) if holding[i] < bound]
        pool, remaining = sum([weights[i] for i in candidates]), rest
        for i in candidates:
            addition = min(bound - holding[i], max(1, remaining * weights[i] // pool), rest)
            holding[i] = holding[i] + addition
            rest = rest - addition
    return np.array(holding)


def normal_values(own_key, shape, spread, limit, pieces=(), kind=jnp.bfloat16):
    array = jax.random.normal(own_key, shape, jnp.float32) * spread
    if len(pieces) > 0:
        array = level_of(own_key, shape, pieces, -0.22, 0.18) * array
    return jnp.clip(array, min=-limit, max=limit).astype(kind)


def setup_inputs(seed: int = 0) -> dict:
    arg_keys = jax.random.split(jax.random.key(seed), 8)
    gas_fields = draw_gas_fields(jax.random.fold_in(arg_keys[7], 71), 0)
    orbit_shift = place_ends(jax.random.randint(arg_keys[1], (NR,), 0, NPHI), jax.random.fold_in(arg_keys[1], 1), 0, NPHI - 1).astype(jnp.int32)
    particle_velocity = normal_values(arg_keys[2], (3, NPART), 1.0, 6.0, ((1, 32),), jnp.float32)
    particle_mass = jnp.clip(jnp.exp(math.log(2.0) - 2.3025851 * jax.random.uniform(arg_keys[3], (NPART,), jnp.float32) ** level_of(arg_keys[3], (NPART,), ((0, 32),), -0.2, 0.2)), 0.2, 2.0)
    particle_stop = jnp.clip(jnp.exp(math.log(10.0) - 4.6051702 * jax.random.uniform(arg_keys[4], (NPART,), jnp.float32) ** level_of(arg_keys[4], (NPART,), ((0, 32),), -0.2, 0.2)), 0.1, 10.0)
    particle_cell = place_ends(jax.random.randint(arg_keys[5], (NPART,), 0, CR * ZL * CP), jax.random.fold_in(arg_keys[5], 1), 0, (CR * ZL * CP) - 1).astype(jnp.int32)
    particle_dest_keys = jax.random.split(jax.random.fold_in(arg_keys[6], 1), NPART // PD)
    particle_dest_turns = jax.random.permutation(jax.random.fold_in(arg_keys[6], 3), NPART // PD)
    particle_dest = jax.vmap(lambda own, number: routed_block(jax.random.fold_in(arg_keys[6], 2), own, number, PD, DEVICES, 1, CAP, 2))(particle_dest_keys, particle_dest_turns).reshape((NPART, 1))
    return dict(gas_fields=gas_fields, orbit_shift=orbit_shift, particle_velocity=particle_velocity, particle_mass=particle_mass, particle_stop=particle_stop, particle_cell=particle_cell, particle_dest=particle_dest)


sound_speed = 1.0
radial_rate = 0.2
azimuth_rate = 0.2


def limited_slope(left_step, right_step):
    return 0.5 * (jnp.sign(left_step) + jnp.sign(right_step)) * jnp.minimum(jnp.abs(left_step), jnp.abs(right_step))


def plm_divergence(values, speed, along_axis, extent):
    def take_range(source, offset_at, length):
        return lax.slice_in_dim(source, offset_at, offset_at + length, axis=along_axis)

    left_step = take_range(values, 1, extent + 2) - take_range(values, 0, extent + 2)
    right_step = take_range(values, 2, extent + 2) - take_range(values, 1, extent + 2)
    slopes = limited_slope(left_step, right_step)
    centre = take_range(values, 1, extent + 2)
    left_value = take_range(centre, 0, extent + 1) + 0.5 * take_range(slopes, 0, extent + 1)
    right_value = take_range(centre, 1, extent + 1) - 0.5 * take_range(slopes, 1, extent + 1)
    face_speed = 0.5 * (take_range(speed, 1, extent + 1) + take_range(speed, 2, extent + 1))
    face_flux = face_speed * 0.5 * (left_value + right_value) - 0.5 * (jnp.abs(face_speed) + sound_speed) * (right_value - left_value)
    return take_range(face_flux, 1, extent) - take_range(face_flux, 0, extent)


def reference(gas_fields, orbit_shift, particle_velocity, particle_mass, particle_stop, particle_cell, particle_dest):
    azimuth = jnp.arange(NPHI, dtype=jnp.int32)
    source_cell = (azimuth[None, :] - orbit_shift[:, None]) % NPHI
    gather_index = jnp.broadcast_to(source_cell[None, :, None, :], gas_fields.shape).astype(jnp.int32)
    shifted = jnp.take_along_axis(gas_fields, gather_index, axis=3)

    records = jnp.concatenate([particle_velocity, particle_mass[None], particle_stop[None], particle_cell[None].astype(jnp.float32)], axis=0)
    record_sets = records.reshape(6, DEVICES, PD).transpose(1, 0, 2)
    target_sets = particle_dest[:, 0].reshape(DEVICES, PD)

    def pack_outbox(pair):
        record_block, target_block = pair
        hits = (target_block[:, None] == jnp.arange(DEVICES, dtype=jnp.int32)[None, :]).astype(jnp.int32)
        slot = jnp.sum(jnp.cumsum(hits, axis=0) * hits, axis=1) - 1
        return jnp.zeros((6, DEVICES, CAP), jnp.float32).at[:, target_block, slot].set(record_block)

    outboxes = lax.map(pack_outbox, (record_sets, target_sets))
    arrived = outboxes.transpose(2, 1, 0, 3).reshape(DEVICES, 6, DEVICES * CAP)
    cells = arrived[:, 5].astype(jnp.int32)
    owner = jnp.arange(DEVICES, dtype=jnp.int32)
    row_local = cells // CP
    radius = (owner // N_SEC)[:, None] * CR + row_local // ZL
    layer = row_local % ZL
    angle_cell = (owner % N_SEC)[:, None] * CP + cells % CP
    velocity = shifted[1:4] / shifted[0:1]
    local_speed = velocity[:, radius, layer, angle_cell]
    fraction = arrived[:, 4] / (1.0 + arrived[:, 4])
    incoming = arrived[:, 0:3].transpose(1, 0, 2)
    change = (incoming - local_speed) * fraction[None]
    arrived_velocity = (incoming - change).reshape(3, DEVICES * DEVICES * CAP)
    impulse = arrived[:, 3][None] * change
    deposit = jnp.zeros((3, NR, ZL, NPHI), jnp.float32).at[:, radius, layer, angle_cell].add(impulse)
    dragged = jnp.concatenate([shifted[0:1], shifted[1:4] + deposit, shifted[4:5]], axis=0)

    radial_speed = dragged[1] / dragged[0]
    azimuthal_speed = dragged[2] / dragged[0]
    radial_pad = jnp.pad(dragged, ((0, 0), (2, 2), (0, 0), (0, 0)))
    radial_speed_pad = jnp.pad(radial_speed, ((2, 2), (0, 0), (0, 0)))
    azimuth_pad = jnp.pad(dragged, ((0, 0), (0, 0), (0, 0), (2, 2)), mode="wrap")
    azimuth_speed_pad = jnp.pad(azimuthal_speed, ((0, 0), (0, 0), (2, 2)), mode="wrap")

    def radial_field(values):
        return plm_divergence(values[None], radial_speed_pad[None], 1, NR)[0]

    def azimuth_field(values):
        return plm_divergence(values[None], azimuth_speed_pad[None], 3, NPHI)[0]

    radial_change = lax.map(radial_field, radial_pad)
    azimuth_change = lax.map(azimuth_field, azimuth_pad)
    gas_next = dragged - radial_rate * radial_change - azimuth_rate * azimuth_change
    return gas_next, arrived_velocity
```

```python
import functools
import jax
import jax.numpy as jnp
from jax import lax
from jax.experimental import pallas as pl
from jax.experimental.pallas import tpu as pltpu
from jax.sharding import PartitionSpec as P

sound_speed = 1.0
radial_rate = 0.2
azimuth_rate = 0.2
MESH = pl.DeviceIdType.MESH
VMEM_LIMIT = 48 * 1024 * 1024
in_vmem = pl.BlockSpec(memory_space=pltpu.VMEM)
in_smem = pl.BlockSpec(memory_space=pltpu.SMEM)


def with_halo(cells, sides, width, closed):
    for axis, dim in sides:
        count = lax.axis_size(axis)
        ends = count if closed else count - 1
        head = lax.slice_in_dim(cells, 0, width, axis=dim)
        tail = lax.slice_in_dim(cells, cells.shape[dim] - width, cells.shape[dim], axis=dim)
        cells = jnp.concatenate(
            [
                lax.ppermute(tail, axis, [(i, (i + 1) % count) for i in range(ends)]),
                cells,
                lax.ppermute(head, axis, [((i + 1) % count, i) for i in range(ends)]),
            ],
            axis=dim,
        )
    return cells


def limited_slope(left_step, right_step):
    return (
        0.5
        * (jnp.sign(left_step) + jnp.sign(right_step))
        * jnp.minimum(jnp.abs(left_step), jnp.abs(right_step))
    )


def plm_divergence(values, speed, along_axis, extent):

    def take_range(source, offset_at, length):
        return lax.slice_in_dim(source, offset_at, offset_at + length, axis=along_axis)

    left_step = take_range(values, 1, extent + 2) - take_range(values, 0, extent + 2)
    right_step = take_range(values, 2, extent + 2) - take_range(values, 1, extent + 2)
    slopes = limited_slope(left_step, right_step)
    centre = take_range(values, 1, extent + 2)
    left_value = take_range(centre, 0, extent + 1) + 0.5 * take_range(slopes, 0, extent + 1)
    right_value = take_range(centre, 1, extent + 1) - 0.5 * take_range(slopes, 1, extent + 1)
    face_speed = 0.5 * (take_range(speed, 1, extent + 1) + take_range(speed, 2, extent + 1))
    face_flux = face_speed * 0.5 * (left_value + right_value) - 0.5 * (
        jnp.abs(face_speed) + sound_speed
    ) * (right_value - left_value)
    return take_range(face_flux, 1, extent) - take_range(face_flux, 0, extent)


def split_terms(x, terms):
    parts = []
    for _ in range(terms):
        part = x.astype(jnp.bfloat16)
        parts.append(part)
        x = x - part.astype(jnp.float32)
    return parts


def pack_kernel(devices, capacity, step, dest_ref, rec_ref, out_ref, acc):
    total = dest_ref.shape[1]
    rows = devices * 8
    upper = (
        lax.broadcasted_iota(jnp.int32, (step, step), 0)
        <= lax.broadcasted_iota(jnp.int32, (step, step), 1)
    ).astype(jnp.float32).astype(jnp.bfloat16)
    acc[...] = jnp.zeros_like(acc)

    def body(i, carry):
        at = pl.ds(pl.multiple_of(i * step, step), step)
        dest = dest_ref[:, at]
        hit = (lax.broadcasted_iota(jnp.int32, (devices, step), 0) == dest).astype(jnp.float32)
        running = (
            jnp.dot(hit.astype(jnp.bfloat16), upper, preferred_element_type=jnp.float32) + carry
        )
        slot = jnp.sum(hit * running, axis=0, keepdims=True).astype(jnp.int32) - 1
        slot_hot = (
            (lax.broadcasted_iota(jnp.int32, (capacity, step), 0) == slot)
            .astype(jnp.float32)
            .astype(jnp.bfloat16)
        )
        hit8 = lax.broadcasted_iota(jnp.int32, (rows, step), 0) // 8 == dest
        rec = rec_ref[:, at]
        for k, part in enumerate(split_terms(rec, 3)):
            tiled = jnp.concatenate([part.astype(jnp.float32)] * devices, axis=0)
            placed = jnp.where(hit8, tiled, 0.0).astype(jnp.bfloat16)
            acc[k * rows : (k + 1) * rows] += lax.dot_general(
                placed, slot_hot, (((1,), (1,)), ((), ())), preferred_element_type=jnp.float32
            )
        return running[:, step - 1 : step]

    lax.fori_loop(0, total // step, body, jnp.zeros((devices, 1), jnp.float32))
    joined = (acc[0:rows] + acc[rows : 2 * rows]) + acc[2 * rows : 3 * rows]
    out_ref[...] = joined.reshape(devices, 8, capacity)


def exchange_kernel(
    slabs,
    sectors,
    shift_ref,
    gas_ref,
    outbox_ref,
    shifted_ref,
    inbox_ref,
    *scratch,
):
    fields, radii, layers, width = gas_ref.shape
    land = scratch[:fields]
    rolled = scratch[fields : 2 * fields]
    send1, recv1, send2, recv2, send3, recv3 = scratch[2 * fields :]
    own = radii // sectors
    devices = slabs * sectors
    rad, sec = lax.axis_index("rad"), lax.axis_index("sec")
    me = rad * sectors + sec

    def place(k):
        peer = lax.rem(me + k, devices)
        return peer, (lax.div(peer, sectors), lax.rem(peer, sectors))

    barrier = pltpu.get_barrier_semaphore()

    def greet(k, _):
        pl.semaphore_signal(barrier, inc=1, device_id=place(k)[1], device_id_type=MESH)
        return 0

    lax.fori_loop(1, devices, greet, 0)
    pl.semaphore_wait(barrier, devices - 1)

    def outward(f, k):
        to = lax.rem(sec + k, sectors)
        return pltpu.make_async_remote_copy(
            src_ref=gas_ref.at[f, pl.ds(to * own, own)],
            dst_ref=land[f].at[sec],
            send_sem=send1.at[f, k],
            recv_sem=recv1.at[f, k],
            device_id=(rad, to),
            device_id_type=MESH,
        )

    def homeward(f, k):
        to = lax.rem(sec + k, sectors)
        return pltpu.make_async_remote_copy(
            src_ref=rolled[f].at[to],
            dst_ref=shifted_ref.at[f, pl.ds(sec * own, own)],
            send_sem=send2.at[f, k],
            recv_sem=recv2.at[f, k],
            device_id=(rad, to),
            device_id_type=MESH,
        )

    def parcel(k):
        peer, where = place(k)
        return pltpu.make_async_remote_copy(
            src_ref=outbox_ref.at[peer],
            dst_ref=inbox_ref.at[me],
            send_sem=send3.at[k],
            recv_sem=recv3.at[k],
            device_id=where,
            device_id_type=MESH,
        )

    def each(first, last, act):
        def body(k, _):
            act(k)
            return 0

        lax.fori_loop(first, last, body, 0)

    for f in range(fields):
        each(1, sectors, lambda k: outward(f, k).start())
    each(1, devices, lambda k: parcel(k).start())
    inbox_ref[me] = outbox_ref[me]
    for f in range(fields):
        land[f][sec] = gas_ref[f, pl.ds(sec * own, own)]
        each(1, sectors, lambda k: outward(f, k).wait_recv())

        def turn(r, _):
            shift = shift_ref[sec * own + r]
            quotient = lax.rem(lax.div(shift, width), sectors)
            rest = lax.rem(shift, width)
            early = lax.broadcasted_iota(jnp.int32, (layers, width), 1) < rest

            def source(t):
                return pltpu.roll(land[f][lax.rem(t - quotient + 2 * sectors, sectors), r], rest, 1)

            def fill(t, before):
                now = source(t)
                rolled[f][t, r] = jnp.where(early, before, now)
                return now

            lax.fori_loop(0, sectors, fill, source(-1))
            return 0

        lax.fori_loop(0, own, turn, 0)
        each(1, sectors, lambda k: homeward(f, k).start())
        shifted_ref[f, pl.ds(sec * own, own)] = rolled[f][sec]
    each(1, devices, lambda k: parcel(k).wait())
    for f in range(fields):
        each(1, sectors, lambda k: outward(f, k).wait_send())
    for f in range(fields):
        each(1, sectors, lambda k: homeward(f, k).wait())


def drag_kernel(step, recv_ref, gas_ref, out_ref, dragged_ref, speeds, acc):
    _, rows, width = gas_ref.shape
    total = recv_ref.shape[1]
    for c in range(3):
        turned = (gas_ref[1 + c] / gas_ref[0]).T
        for k, part in enumerate(split_terms(turned, 2)):
            speeds[c * width : (c + 1) * width, k * rows : (k + 1) * rows] = part
    acc[...] = jnp.zeros_like(acc)

    def body(i, _):
        at = pl.ds(pl.multiple_of(i * step, step), step)
        rec = recv_ref[:, at]
        cell = rec[5:6].astype(jnp.int32)
        row, angle = lax.div(cell, width), lax.rem(cell, width)
        row_hot = (
            (lax.broadcasted_iota(jnp.int32, (rows, step), 0) == row)
            .astype(jnp.float32)
            .astype(jnp.bfloat16)
        )
        picked = jnp.dot(
            speeds[...],
            jnp.concatenate([row_hot, row_hot], axis=0),
            preferred_element_type=jnp.float32,
        )
        angle_hot = lax.broadcasted_iota(jnp.int32, (width, step), 0) == angle
        stop = rec[4:5]
        fraction = stop / (1.0 + stop)
        spread = [[], []]
        for c in range(3):
            local = jnp.sum(
                jnp.where(angle_hot, picked[c * width : (c + 1) * width], 0.0),
                axis=0,
                keepdims=True,
            )
            velocity = rec[c : c + 1]
            change = (velocity - local) * fraction
            out_ref[c : c + 1, at] = velocity - change
            for k, part in enumerate(split_terms(rec[3:4] * change, 2)):
                spread[k].append(
                    jnp.where(angle_hot, part.astype(jnp.float32), 0.0).astype(jnp.bfloat16)
                )
        acc[...] += lax.dot_general(
            jnp.concatenate(spread[0] + spread[1], axis=0),
            row_hot,
            (((1,), (1,)), ((), ())),
            preferred_element_type=jnp.float32,
        )
        return 0

    lax.fori_loop(0, total // step, body, 0)
    dragged_ref[0] = gas_ref[0]
    dragged_ref[4] = gas_ref[4]
    for c in range(3):
        added = (
            acc[c * width : (c + 1) * width] + acc[(3 + c) * width : (4 + c) * width]
        )
        dragged_ref[1 + c] = gas_ref[1 + c] + added.T


def local(
    slabs,
    sectors,
    gas_fields,
    orbit_shift,
    particle_velocity,
    particle_mass,
    particle_stop,
    particle_cell,
    particle_dest,
):
    fields, radii, layers, sector = gas_fields.shape
    per_device = particle_dest.shape[0]
    devices = slabs * sectors
    capacity = 2 * per_device // devices
    own = radii // sectors
    rows = radii * layers
    slots = devices * capacity
    records = jnp.concatenate(
        [
            particle_velocity,
            particle_mass[None],
            particle_stop[None],
            particle_cell[None].astype(jnp.float32),
            jnp.zeros((2, per_device), jnp.float32),
        ],
        axis=0,
    )
    limit = pltpu.CompilerParams(vmem_limit_bytes=VMEM_LIMIT)
    outbox = pl.pallas_call(
        functools.partial(pack_kernel, devices, capacity, 512),
        out_shape=jax.ShapeDtypeStruct((devices, 8, capacity), jnp.float32),
        in_specs=[in_vmem, in_vmem],
        out_specs=in_vmem,
        scratch_shapes=[pltpu.VMEM((3 * devices * 8, capacity), jnp.float32)],
        compiler_params=limit,
    )(particle_dest.reshape(1, per_device), records)
    dma = pltpu.SemaphoreType.DMA
    shifted, inbox = pl.pallas_call(
        functools.partial(exchange_kernel, slabs, sectors),
        out_shape=(
            jax.ShapeDtypeStruct(gas_fields.shape, jnp.float32),
            jax.ShapeDtypeStruct((devices, 8, capacity), jnp.float32),
        ),
        in_specs=[in_smem, in_vmem, in_vmem],
        out_specs=(in_vmem, in_vmem),
        scratch_shapes=[pltpu.VMEM((sectors, own, layers, sector), jnp.float32)] * (2 * fields)
        + [dma((fields, sectors))] * 4
        + [dma((devices,))] * 2,
        compiler_params=pltpu.CompilerParams(
            vmem_limit_bytes=VMEM_LIMIT, collective_id=0, has_side_effects=True
        ),
    )(orbit_shift, gas_fields, outbox)
    received = inbox.transpose(1, 0, 2).reshape(8, slots)
    arrived_velocity, dragged = pl.pallas_call(
        functools.partial(drag_kernel, 512),
        out_shape=(
            jax.ShapeDtypeStruct((3, slots), jnp.float32),
            jax.ShapeDtypeStruct((fields, rows, sector), jnp.float32),
        ),
        in_specs=[in_vmem, in_vmem],
        out_specs=(in_vmem, in_vmem),
        scratch_shapes=[
            pltpu.VMEM((3 * sector, 2 * rows), jnp.bfloat16),
            pltpu.VMEM((6 * sector, rows), jnp.float32),
        ],
        compiler_params=limit,
    )(received, shifted.reshape(fields, rows, sector))
    dragged = dragged.reshape(fields, radii, layers, sector)
    radial_speed = dragged[1] / dragged[0]
    azimuthal_speed = dragged[2] / dragged[0]
    stacked = jnp.concatenate([dragged, radial_speed[None], azimuthal_speed[None]], axis=0)
    radial_pad = with_halo(stacked, (("rad", 1),), 2, False)
    azimuth_pad = with_halo(stacked, (("sec", 3),), 2, True)
    radial_change = plm_divergence(radial_pad[0:5], radial_pad[5:6], 1, radii)
    azimuth_change = plm_divergence(azimuth_pad[0:5], azimuth_pad[6:7], 3, sector)
    gas_next = dragged - radial_rate * radial_change - azimuth_rate * azimuth_change
    return (gas_next, arrived_velocity)


def solution(mesh):
    placed = (
        P(None, "rad", None, "sec"),
        P("rad"),
        P(None, ("rad", "sec")),
        P(("rad", "sec")),
        P(("rad", "sec")),
        P(("rad", "sec")),
        P(("rad", "sec"), None),
    )
    return jax.shard_map(
        functools.partial(local, mesh.shape["rad"], mesh.shape["sec"]),
        mesh=mesh,
        in_specs=placed,
        out_specs=(P(None, "rad", None, "sec"), P(None, ("rad", "sec"))),
        check_vma=False,
    )
```

```python
import functools
import jax
import jax.numpy as jnp
from jax import lax
from jax.experimental import pallas as pl
from jax.experimental.pallas import tpu as pltpu
from jax.sharding import PartitionSpec as P

sound_speed = 1.0
radial_rate = 0.2
azimuth_rate = 0.2
MESH = pl.DeviceIdType.MESH
VMEM_LIMIT = 48 * 1024 * 1024
in_vmem = pl.BlockSpec(memory_space=pltpu.VMEM)
in_smem = pl.BlockSpec(memory_space=pltpu.SMEM)


def limited_slope(left_step, right_step):
    rising = jnp.maximum(jnp.minimum(left_step, right_step), 0.0)
    return rising + jnp.minimum(jnp.maximum(left_step, right_step), 0.0)


def face_flux(left_value, right_value, left_speed, right_speed):
    face_speed = 0.5 * (left_speed + right_speed)
    return face_speed * 0.5 * (left_value + right_value) - 0.5 * (
        jnp.abs(face_speed) + sound_speed
    ) * (right_value - left_value)


def leading_divergence(values, speed, extent):
    steps = values[1:] - values[:-1]
    slopes = 0.5 * limited_slope(steps[:-1], steps[1:])
    centre = values[1:-1]
    flux = face_flux(
        centre[:-1] + slopes[:-1],
        centre[1:] - slopes[1:],
        speed[1 : extent + 2],
        speed[2 : extent + 3],
    )
    return flux[1:] - flux[:-1]


def lane_divergence(values, speed, far_left, left, right, far_right, left_speed, right_speed):
    width = values.shape[1]
    lane = lax.broadcasted_iota(jnp.int32, values.shape, 1)
    first, last = lane == 0, lane == width - 1

    def after(x, end):
        return jnp.where(last, end, pltpu.roll(x, width - 1, 1))

    def before(x, start):
        return jnp.where(first, start, pltpu.roll(x, 1, 1))

    head, tail = values[:, 0:1], values[:, width - 1 : width]
    following = after(values, right)
    step = following - values
    slopes = 0.5 * limited_slope(before(step, head - left), step)
    end_slope = 0.5 * limited_slope(right - tail, far_right - right)
    start_slope = 0.5 * limited_slope(left - far_left, head - left)
    flux = face_flux(
        values + slopes,
        following - after(slopes, end_slope),
        speed,
        after(speed, right_speed),
    )
    start_flux = face_flux(
        left + start_slope, head - slopes[:, 0:1], left_speed, speed[:, 0:1]
    )
    return flux - before(flux, start_flux)


def split_terms(x, terms):
    parts = []
    for _ in range(terms):
        part = x.astype(jnp.bfloat16)
        parts.append(part)
        x = x - part.astype(jnp.float32)
    return parts


def pack_kernel(devices, capacity, step, dest_ref, rec_ref, out_ref, acc):
    total = dest_ref.shape[1]
    rows = devices * 8
    upper = (
        lax.broadcasted_iota(jnp.int32, (step, step), 0)
        <= lax.broadcasted_iota(jnp.int32, (step, step), 1)
    ).astype(jnp.float32).astype(jnp.bfloat16)
    acc[...] = jnp.zeros_like(acc)

    def body(i, carry):
        at = pl.ds(pl.multiple_of(i * step, step), step)
        dest = dest_ref[:, at]
        hit = (lax.broadcasted_iota(jnp.int32, (devices, step), 0) == dest).astype(jnp.float32)
        running = (
            jnp.dot(hit.astype(jnp.bfloat16), upper, preferred_element_type=jnp.float32) + carry
        )
        slot = jnp.sum(hit * running, axis=0, keepdims=True).astype(jnp.int32) - 1
        slot_hot = (
            (lax.broadcasted_iota(jnp.int32, (capacity, step), 0) == slot)
            .astype(jnp.float32)
            .astype(jnp.bfloat16)
        )
        hit8 = lax.broadcasted_iota(jnp.int32, (rows, step), 0) // 8 == dest
        rec = rec_ref[:, at]
        for k, part in enumerate(split_terms(rec, 3)):
            tiled = jnp.concatenate([part.astype(jnp.float32)] * devices, axis=0)
            placed = jnp.where(hit8, tiled, 0.0).astype(jnp.bfloat16)
            acc[k * rows : (k + 1) * rows] += lax.dot_general(
                placed, slot_hot, (((1,), (1,)), ((), ())), preferred_element_type=jnp.float32
            )
        return running[:, step - 1 : step]

    lax.fori_loop(0, total // step, body, jnp.zeros((devices, 1), jnp.float32))
    joined = (acc[0:rows] + acc[rows : 2 * rows]) + acc[2 * rows : 3 * rows]
    out_ref[...] = joined.reshape(devices, 8, capacity)


def step_kernel(
    slabs,
    sectors,
    step,
    shift_ref,
    gas_ref,
    dest_ref,
    rec_ref,
    padded_ref,
    out_ref,
    low_ref,
    high_ref,
    *scratch,
):
    fields, radii, layers, width = gas_ref.shape
    land = scratch[:fields]
    rolled = scratch[fields : 2 * fields]
    outbox, inbox, pack_acc, speeds, acc, low_edge, high_edge = scratch[2 * fields : 2 * fields + 7]
    send1, recv1, send2, recv2, send3, recv3, send4, recv4 = scratch[2 * fields + 7 :]
    own = radii // sectors
    rows = radii * layers
    devices = slabs * sectors
    capacity = outbox.shape[2]
    rad, sec = lax.axis_index("rad"), lax.axis_index("sec")
    me = rad * sectors + sec

    def place(k):
        peer = lax.rem(me + k, devices)
        return peer, (lax.div(peer, sectors), lax.rem(peer, sectors))

    barrier = pltpu.get_barrier_semaphore()

    def greet(k, _):
        pl.semaphore_signal(barrier, inc=1, device_id=place(k)[1], device_id_type=MESH)
        return 0

    lax.fori_loop(1, devices, greet, 0)
    pl.semaphore_wait(barrier, devices - 1)

    def outward(f, k):
        to = lax.rem(sec + k, sectors)
        return pltpu.make_async_remote_copy(
            src_ref=gas_ref.at[f, pl.ds(to * own, own)],
            dst_ref=land[f].at[sec],
            send_sem=send1.at[f, k],
            recv_sem=recv1.at[f, k],
            device_id=(rad, to),
            device_id_type=MESH,
        )

    def homeward(f, k):
        to = lax.rem(sec + k, sectors)
        return pltpu.make_async_remote_copy(
            src_ref=rolled[f].at[to],
            dst_ref=padded_ref.at[f, pl.ds(2 + sec * own, own)],
            send_sem=send2.at[f, k],
            recv_sem=recv2.at[f, k],
            device_id=(rad, to),
            device_id_type=MESH,
        )

    def parcel(k):
        peer, where = place(k)
        return pltpu.make_async_remote_copy(
            src_ref=outbox.at[peer],
            dst_ref=inbox.at[me],
            send_sem=send3.at[k],
            recv_sem=recv3.at[k],
            device_id=where,
            device_id_type=MESH,
        )

    def each(first, last, act):
        def body(k, _):
            act(k)
            return 0

        lax.fori_loop(first, last, body, 0)

    def turn_field(f):
        land[f][sec] = gas_ref[f, pl.ds(sec * own, own)]
        each(1, sectors, lambda k: outward(f, k).wait_recv())

        def turn(r, _):
            shift = shift_ref[sec * own + r]
            quotient = lax.rem(lax.div(shift, width), sectors)
            rest = lax.rem(shift, width)
            early = lax.broadcasted_iota(jnp.int32, (layers, width), 1) < rest

            def source(t):
                return pltpu.roll(land[f][lax.rem(t - quotient + 2 * sectors, sectors), r], rest, 1)

            def fill(t, before):
                now = source(t)
                rolled[f][t, r] = jnp.where(early, before, now)
                return now

            lax.fori_loop(0, sectors, fill, source(-1))
            return 0

        lax.fori_loop(0, own, turn, 0)
        each(1, sectors, lambda k: homeward(f, k).start())
        padded_ref[f, pl.ds(2 + sec * own, own)] = rolled[f][sec]

    def field(f):
        return padded_ref[f, 2 : 2 + radii].reshape(rows, width)

    energy = fields - 1
    for f in range(energy):
        each(1, sectors, lambda k: outward(f, k).start())
    pack_kernel(devices, capacity, step, dest_ref, rec_ref, outbox, pack_acc)
    each(1, devices, lambda k: parcel(k).start())
    inbox[me] = outbox[me]
    for f in range(energy):
        turn_field(f)
    for f in range(energy):
        if f == energy - 1:
            each(1, sectors, lambda k: outward(energy, k).start())
        each(1, sectors, lambda k: homeward(f, k).wait_recv())
    each(1, devices, lambda k: parcel(k).wait())

    for c in range(3):
        turned = (field(1 + c) / field(0)).T
        for k, part in enumerate(split_terms(turned, 2)):
            speeds[c * width : (c + 1) * width, k * rows : (k + 1) * rows] = part
    acc[...] = jnp.zeros_like(acc)
    group = step // capacity

    def drag(i, _):
        at = pl.ds(pl.multiple_of(i * step, step), step)
        rec = jnp.concatenate([inbox[i * group + j] for j in range(group)], axis=1)
        cell = rec[5:6].astype(jnp.int32)
        row, angle = lax.div(cell, width), lax.rem(cell, width)
        row_hot = (
            (lax.broadcasted_iota(jnp.int32, (rows, step), 0) == row)
            .astype(jnp.float32)
            .astype(jnp.bfloat16)
        )
        picked = jnp.dot(
            speeds[...],
            jnp.concatenate([row_hot, row_hot], axis=0),
            preferred_element_type=jnp.float32,
        )
        angle_hot = lax.broadcasted_iota(jnp.int32, (width, step), 0) == angle
        stop = rec[4:5]
        fraction = stop / (1.0 + stop)
        spread = [[], []]
        for c in range(3):
            local_speed = jnp.sum(
                jnp.where(angle_hot, picked[c * width : (c + 1) * width], 0.0),
                axis=0,
                keepdims=True,
            )
            velocity = rec[c : c + 1]
            change = (velocity - local_speed) * fraction
            out_ref[c : c + 1, at] = velocity - change
            for k, part in enumerate(split_terms(rec[3:4] * change, 2)):
                spread[k].append(
                    jnp.where(angle_hot, part.astype(jnp.float32), 0.0).astype(jnp.bfloat16)
                )
        acc[...] += lax.dot_general(
            jnp.concatenate(spread[0] + spread[1], axis=0),
            row_hot,
            (((1,), (1,)), ((), ())),
            preferred_element_type=jnp.float32,
        )
        return 0

    blocks = devices * capacity // step
    lax.fori_loop(0, blocks // 2, drag, 0)
    turn_field(energy)
    lax.fori_loop(blocks // 2, blocks, drag, 0)
    for c in range(3):
        added = acc[c * width : (c + 1) * width] + acc[(3 + c) * width : (4 + c) * width]
        total = field(1 + c) + added.T
        padded_ref[1 + c, 2 : 2 + radii] = total.reshape(radii, layers, width)
    each(1, sectors, lambda k: homeward(energy, k).wait_recv())

    for f in range(fields):
        whole = field(f)
        low_edge[f] = whole[:, 0:128].T[0:8]
        high_edge[f] = whole[:, width - 128 : width].T[120:128]
    up, down = lax.rem(rad + 1, slabs), lax.rem(rad + slabs - 1, slabs)
    east, west = lax.rem(sec + 1, sectors), lax.rem(sec + sectors - 1, sectors)
    halos = []
    for n, (src, dst, where) in enumerate(
        [
            (padded_ref.at[:, 2:4], padded_ref.at[:, 2 + radii : 4 + radii], (down, sec)),
            (padded_ref.at[:, radii : 2 + radii], padded_ref.at[:, 0:2], (up, sec)),
            (low_edge, high_ref, (rad, west)),
            (high_edge, low_ref, (rad, east)),
        ]
    ):
        halos.append(
            pltpu.make_async_remote_copy(
                src_ref=src,
                dst_ref=dst,
                send_sem=send4.at[n],
                recv_sem=recv4.at[n],
                device_id=where,
                device_id_type=MESH,
            )
        )
    for copy in halos:
        copy.start()
    for f in range(fields):
        each(1, sectors, lambda k: outward(f, k).wait_send())
        each(1, sectors, lambda k: homeward(f, k).wait_send())
    for copy in halos:
        copy.wait()

    @pl.when(rad == 0)
    def _():
        padded_ref[:, 0:2] = jnp.zeros((fields, 2, layers, width), jnp.float32)

    @pl.when(rad == slabs - 1)
    def _():
        padded_ref[:, 2 + radii : 4 + radii] = jnp.zeros((fields, 2, layers, width), jnp.float32)


def transport_kernel(chunk, padded_ref, low_ref, high_ref, next_ref, sides):
    fields, radii, layers, width = next_ref.shape
    rows = chunk * layers
    for f in range(fields):
        sides[f] = jnp.concatenate([high_ref[f], low_ref[f]] * 8, axis=0).T

    def body(i, _):
        r = i * chunk
        density = padded_ref[0, pl.ds(r, chunk + 4)]
        density = jnp.where(density == 0.0, 1.0, density)
        radial_speed = padded_ref[1, pl.ds(r, chunk + 4)] / density
        speed = (padded_ref[2, pl.ds(r + 2, chunk)] / density[2 : 2 + chunk]).reshape(rows, width)
        at = pl.ds(pl.multiple_of(r * layers, rows), rows)
        end_speed = sides[2, at] / sides[0, at]
        for f in range(fields):
            values = padded_ref[f, pl.ds(r, chunk + 4)]
            centre = values[2 : 2 + chunk]
            side = sides[f, at]
            along = lane_divergence(
                centre.reshape(rows, width),
                speed,
                side[:, 14:15],
                side[:, 15:16],
                side[:, 0:1],
                side[:, 1:2],
                end_speed[:, 15:16],
                end_speed[:, 0:1],
            ).reshape(chunk, layers, width)
            across = leading_divergence(values, radial_speed, chunk)
            next_ref[f, pl.ds(r, chunk)] = centre - radial_rate * across - azimuth_rate * along
        return 0

    lax.fori_loop(0, radii // chunk, body, 0)


def local(
    slabs,
    sectors,
    gas_fields,
    orbit_shift,
    particle_velocity,
    particle_mass,
    particle_stop,
    particle_cell,
    particle_dest,
):
    fields, radii, layers, sector = gas_fields.shape
    per_device = particle_dest.shape[0]
    devices = slabs * sectors
    capacity = 2 * per_device // devices
    own = radii // sectors
    rows = radii * layers
    slots = devices * capacity
    records = jnp.concatenate(
        [
            particle_velocity,
            particle_mass[None],
            particle_stop[None],
            particle_cell[None].astype(jnp.float32),
            jnp.zeros((2, per_device), jnp.float32),
        ],
        axis=0,
    )
    step = 512
    f32 = jnp.float32
    dma = pltpu.SemaphoreType.DMA
    padded, arrived_velocity, low, high = pl.pallas_call(
        functools.partial(step_kernel, slabs, sectors, step),
        out_shape=(
            jax.ShapeDtypeStruct((fields, radii + 4, layers, sector), f32),
            jax.ShapeDtypeStruct((3, slots), f32),
            jax.ShapeDtypeStruct((fields, 8, rows), f32),
            jax.ShapeDtypeStruct((fields, 8, rows), f32),
        ),
        in_specs=[in_smem] + [in_vmem] * 3,
        out_specs=(in_vmem,) * 4,
        scratch_shapes=[pltpu.VMEM((sectors, own, layers, sector), f32)] * (2 * fields)
        + [
            pltpu.VMEM((devices, 8, capacity), f32),
            pltpu.VMEM((devices, 8, capacity), f32),
            pltpu.VMEM((3 * devices * 8, capacity), f32),
            pltpu.VMEM((3 * sector, 2 * rows), jnp.bfloat16),
            pltpu.VMEM((6 * sector, rows), f32),
            pltpu.VMEM((fields, 8, rows), f32),
            pltpu.VMEM((fields, 8, rows), f32),
        ]
        + [dma((fields, sectors))] * 4
        + [dma((devices,))] * 2
        + [dma((4,))] * 2,
        compiler_params=pltpu.CompilerParams(
            vmem_limit_bytes=VMEM_LIMIT, collective_id=0, has_side_effects=True
        ),
    )(orbit_shift, gas_fields, particle_dest.reshape(1, per_device), records)
    gas_next = pl.pallas_call(
        functools.partial(transport_kernel, 4),
        out_shape=jax.ShapeDtypeStruct(gas_fields.shape, f32),
        in_specs=[in_vmem] * 3,
        out_specs=in_vmem,
        scratch_shapes=[pltpu.VMEM((fields, rows, 128), f32)],
        compiler_params=pltpu.CompilerParams(vmem_limit_bytes=VMEM_LIMIT),
    )(padded, low, high)
    return (gas_next, arrived_velocity)


def solution(mesh):
    placed = (
        P(None, "rad", None, "sec"),
        P("rad"),
        P(None, ("rad", "sec")),
        P(("rad", "sec")),
        P(("rad", "sec")),
        P(("rad", "sec")),
        P(("rad", "sec"), None),
    )
    return jax.shard_map(
        functools.partial(local, mesh.shape["rad"], mesh.shape["sec"]),
        mesh=mesh,
        in_specs=placed,
        out_specs=(P(None, "rad", None, "sec"), P(None, ("rad", "sec"))),
        check_vma=False,
    )
```

```python
import functools
import jax
import jax.numpy as jnp
from jax import lax
from jax.experimental import pallas as pl
from jax.experimental.pallas import tpu as pltpu
from jax.sharding import PartitionSpec as P

sound_speed = 1.0
radial_rate = 0.2
azimuth_rate = 0.2
MESH = pl.DeviceIdType.MESH
VMEM_LIMIT = 48 * 1024 * 1024
in_vmem = pl.BlockSpec(memory_space=pltpu.VMEM)
in_smem = pl.BlockSpec(memory_space=pltpu.SMEM)


def limited_slope(left_step, right_step):
    rising = jnp.maximum(jnp.minimum(left_step, right_step), 0.0)
    return rising + jnp.minimum(jnp.maximum(left_step, right_step), 0.0)


def face_weights(left_speed, right_speed):
    face_speed = 0.5 * (left_speed + right_speed)
    return face_speed * 0.5, 0.5 * (jnp.abs(face_speed) + sound_speed)


def face_flux(left_value, right_value, weights):
    return weights[0] * (left_value + right_value) - weights[1] * (right_value - left_value)


def leading_divergence(values, weights):
    steps = values[1:] - values[:-1]
    slopes = 0.5 * limited_slope(steps[:-1], steps[1:])
    centre = values[1:-1]
    flux = face_flux(centre[:-1] + slopes[:-1], centre[1:] - slopes[1:], weights)
    return flux[1:] - flux[:-1]


def lane_divergence(values, weights, first_step, last_step, first_flux, last_flux):
    width = values.shape[1]
    lane = lax.broadcasted_iota(jnp.int32, values.shape, 1)
    first, last = lane == 0, lane == width - 1

    def before(x, start):
        return jnp.where(first, start, pltpu.roll(x, 1, 1))

    step = jnp.where(last, last_step, pltpu.roll(values, width - 1, 1) - values)
    slopes = 0.5 * limited_slope(before(step, first_step), step)
    flux = face_flux(values + slopes, pltpu.roll(values - slopes, width - 1, 1), weights)
    flux = jnp.where(last, last_flux, flux)
    return flux - before(flux, first_flux)


def boundary_flux(far_left, left, right, far_right, weights):
    step = right - left
    left_slope = 0.5 * limited_slope(left - far_left, step)
    right_slope = 0.5 * limited_slope(step, far_right - right)
    return step, face_flux(left + left_slope, right - right_slope, weights)


def split_terms(x, terms):
    parts = []
    for _ in range(terms):
        part = x.astype(jnp.bfloat16)
        parts.append(part)
        x = x - part.astype(jnp.float32)
    return parts


def pack_kernel(devices, capacity, step, dest_ref, rec_ref, out_ref, acc):
    total = dest_ref.shape[1]
    rows = devices * 8
    upper = (
        lax.broadcasted_iota(jnp.int32, (step, step), 0)
        <= lax.broadcasted_iota(jnp.int32, (step, step), 1)
    ).astype(jnp.float32).astype(jnp.bfloat16)
    acc[...] = jnp.zeros_like(acc)

    def body(i, carry):
        at = pl.ds(pl.multiple_of(i * step, step), step)
        dest = dest_ref[:, at]
        hit = (lax.broadcasted_iota(jnp.int32, (devices, step), 0) == dest).astype(jnp.float32)
        running = (
            jnp.dot(hit.astype(jnp.bfloat16), upper, preferred_element_type=jnp.float32) + carry
        )
        slot = jnp.sum(hit * running, axis=0, keepdims=True).astype(jnp.int32) - 1
        slot_hot = (
            (lax.broadcasted_iota(jnp.int32, (capacity, step), 0) == slot)
            .astype(jnp.float32)
            .astype(jnp.bfloat16)
        )
        hit8 = lax.broadcasted_iota(jnp.int32, (rows, step), 0) // 8 == dest
        rec = rec_ref[:, at]
        for k, part in enumerate(split_terms(rec, 3)):
            tiled = jnp.concatenate([part.astype(jnp.float32)] * devices, axis=0)
            placed = jnp.where(hit8, tiled, 0.0).astype(jnp.bfloat16)
            acc[k * rows : (k + 1) * rows] += lax.dot_general(
                placed, slot_hot, (((1,), (1,)), ((), ())), preferred_element_type=jnp.float32
            )
        return running[:, step - 1 : step]

    lax.fori_loop(0, total // step, body, jnp.zeros((devices, 1), jnp.float32))
    joined = (acc[0:rows] + acc[rows : 2 * rows]) + acc[2 * rows : 3 * rows]
    out_ref[...] = joined.reshape(devices, 8, capacity)


def step_kernel(
    slabs,
    sectors,
    step,
    shift_ref,
    gas_ref,
    dest_ref,
    rec_ref,
    padded_ref,
    out_ref,
    low_ref,
    high_ref,
    low_edge,
    high_edge,
    *scratch,
):
    fields, radii, layers, width = gas_ref.shape
    land = scratch[:fields]
    rolled = scratch[fields : 2 * fields]
    outbox, inbox, pack_acc, speeds, acc = scratch[2 * fields : 2 * fields + 5]
    send1, recv1, send2, recv2, send3, recv3, send4, recv4 = scratch[2 * fields + 5 :]
    own = radii // sectors
    rows = radii * layers
    devices = slabs * sectors
    capacity = outbox.shape[2]
    rad, sec = lax.axis_index("rad"), lax.axis_index("sec")
    me = rad * sectors + sec

    def place(k):
        peer = lax.rem(me + k, devices)
        return peer, (lax.div(peer, sectors), lax.rem(peer, sectors))

    barrier = pltpu.get_barrier_semaphore()

    def greet(k, _):
        pl.semaphore_signal(barrier, inc=1, device_id=place(k)[1], device_id_type=MESH)
        return 0

    lax.fori_loop(1, devices, greet, 0)
    pl.semaphore_wait(barrier, devices - 1)

    def outward(f, k):
        to = lax.rem(sec + k, sectors)
        return pltpu.make_async_remote_copy(
            src_ref=gas_ref.at[f, pl.ds(to * own, own)],
            dst_ref=land[f].at[sec],
            send_sem=send1.at[f, k],
            recv_sem=recv1.at[f, k],
            device_id=(rad, to),
            device_id_type=MESH,
        )

    def homeward(f, k):
        to = lax.rem(sec + k, sectors)
        return pltpu.make_async_remote_copy(
            src_ref=rolled[f].at[to],
            dst_ref=padded_ref.at[f, pl.ds(2 + sec * own, own)],
            send_sem=send2.at[f, k],
            recv_sem=recv2.at[f, k],
            device_id=(rad, to),
            device_id_type=MESH,
        )

    def parcel(k):
        peer, where = place(k)
        return pltpu.make_async_remote_copy(
            src_ref=outbox.at[peer],
            dst_ref=inbox.at[me],
            send_sem=send3.at[k],
            recv_sem=recv3.at[k],
            device_id=where,
            device_id_type=MESH,
        )

    def each(first, last, act):
        def body(k, _):
            act(k)
            return 0

        lax.fori_loop(first, last, body, 0)

    def turn_field(f):
        land[f][sec] = gas_ref[f, pl.ds(sec * own, own)]
        each(1, sectors, lambda k: outward(f, k).wait_recv())

        def turn(r, _):
            shift = shift_ref[sec * own + r]
            quotient = lax.rem(lax.div(shift, width), sectors)
            rest = lax.rem(shift, width)
            early = lax.broadcasted_iota(jnp.int32, (layers, width), 1) < rest

            def source(t):
                return pltpu.roll(land[f][lax.rem(t - quotient + 2 * sectors, sectors), r], rest, 1)

            def fill(t, before):
                now = source(t)
                rolled[f][t, r] = jnp.where(early, before, now)
                return now

            lax.fori_loop(0, sectors, fill, source(-1))
            return 0

        lax.fori_loop(0, own, turn, 0)
        each(1, sectors, lambda k: homeward(f, k).start())
        padded_ref[f, pl.ds(2 + sec * own, own)] = rolled[f][sec]

    def field(f):
        return padded_ref[f, 2 : 2 + radii].reshape(rows, width)

    energy = fields - 1
    for f in range(energy):
        each(1, sectors, lambda k: outward(f, k).start())
    pack_kernel(devices, capacity, step, dest_ref, rec_ref, outbox, pack_acc)
    each(1, devices, lambda k: parcel(k).start())
    inbox[me] = outbox[me]
    for f in range(energy):
        turn_field(f)
    for f in range(energy):
        if f == energy - 1:
            each(1, sectors, lambda k: outward(energy, k).start())
        each(1, sectors, lambda k: homeward(f, k).wait_recv())
    each(1, devices, lambda k: parcel(k).wait())

    for c in range(3):
        turned = (field(1 + c) / field(0)).T
        for k, part in enumerate(split_terms(turned, 2)):
            speeds[c * width : (c + 1) * width, k * rows : (k + 1) * rows] = part
    acc[...] = jnp.zeros_like(acc)
    step = 2 * step
    group = step // capacity

    def drag(i, _):
        at = pl.ds(pl.multiple_of(i * step, step), step)
        rec = jnp.concatenate([inbox[i * group + j] for j in range(group)], axis=1)
        cell = rec[5:6].astype(jnp.int32)
        row, angle = lax.div(cell, width), lax.rem(cell, width)
        row_hot = (
            (lax.broadcasted_iota(jnp.int32, (rows, step), 0) == row)
            .astype(jnp.float32)
            .astype(jnp.bfloat16)
        )
        picked = jnp.dot(
            speeds[...],
            jnp.concatenate([row_hot, row_hot], axis=0),
            preferred_element_type=jnp.float32,
        )
        angle_hot = lax.broadcasted_iota(jnp.int32, (width, step), 0) == angle
        stop = rec[4:5]
        fraction = stop / (1.0 + stop)
        spread = [[], []]
        for c in range(3):
            local_speed = jnp.sum(
                jnp.where(angle_hot, picked[c * width : (c + 1) * width], 0.0),
                axis=0,
                keepdims=True,
            )
            velocity = rec[c : c + 1]
            change = (velocity - local_speed) * fraction
            out_ref[c : c + 1, at] = velocity - change
            for k, part in enumerate(split_terms(rec[3:4] * change, 2)):
                spread[k].append(
                    jnp.where(angle_hot, part.astype(jnp.float32), 0.0).astype(jnp.bfloat16)
                )
        acc[...] += lax.dot_general(
            jnp.concatenate(spread[0] + spread[1], axis=0),
            row_hot,
            (((1,), (1,)), ((), ())),
            preferred_element_type=jnp.float32,
        )
        return 0

    blocks = devices * capacity // step
    lax.fori_loop(0, blocks // 2, drag, 0)
    turn_field(energy)
    lax.fori_loop(blocks // 2, blocks, drag, 0)
    for c in range(3):
        added = acc[c * width : (c + 1) * width] + acc[(3 + c) * width : (4 + c) * width]
        total = field(1 + c) + added.T
        padded_ref[1 + c, 2 : 2 + radii] = total.reshape(radii, layers, width)
    each(1, sectors, lambda k: homeward(energy, k).wait_recv())

    for f in range(fields):
        whole = field(f)
        low_edge[f] = whole[:, 0:128].T[0:8]
        high_edge[f] = whole[:, width - 128 : width].T[120:128]
    up, down = lax.rem(rad + 1, slabs), lax.rem(rad + slabs - 1, slabs)
    east, west = lax.rem(sec + 1, sectors), lax.rem(sec + sectors - 1, sectors)
    halos = []
    for n, (src, dst, where) in enumerate(
        [
            (padded_ref.at[:, 2:4], padded_ref.at[:, 2 + radii : 4 + radii], (down, sec)),
            (padded_ref.at[:, radii : 2 + radii], padded_ref.at[:, 0:2], (up, sec)),
            (low_edge, high_ref, (rad, west)),
            (high_edge, low_ref, (rad, east)),
        ]
    ):
        halos.append(
            pltpu.make_async_remote_copy(
                src_ref=src,
                dst_ref=dst,
                send_sem=send4.at[n],
                recv_sem=recv4.at[n],
                device_id=where,
                device_id_type=MESH,
            )
        )
    for copy in halos:
        copy.start()
    for f in range(fields):
        each(1, sectors, lambda k: outward(f, k).wait_send())
        each(1, sectors, lambda k: homeward(f, k).wait_send())
    for copy in halos:
        copy.wait()

    @pl.when(rad == 0)
    def _():
        padded_ref[:, 0:2] = jnp.zeros((fields, 2, layers, width), jnp.float32)

    @pl.when(rad == slabs - 1)
    def _():
        padded_ref[:, 2 + radii : 4 + radii] = jnp.zeros((fields, 2, layers, width), jnp.float32)


def transport_kernel(chunk, padded_ref, low_ref, high_ref, own_low, own_high, next_ref, sides):
    fields, radii, layers, width = next_ref.shape
    rows = chunk * layers

    def cells(f):
        west, east, head, tail = low_ref[f], high_ref[f], own_low[f], own_high[f]
        return (west[6:7], west[7:8], head[0:1], head[1:2]), (
            tail[6:7],
            tail[7:8],
            east[0:1],
            east[1:2],
        )

    def boundary_weights(side):
        density, momentum = cells(0)[side], cells(2)[side]
        return face_weights(momentum[1] / density[1], momentum[2] / density[2])

    pieces = []
    for f in range(fields):
        for side in range(2):
            pieces += boundary_flux(*cells(f)[side], boundary_weights(side))
    filler = jnp.zeros((128 - len(pieces), radii * layers), jnp.float32)
    sides[...] = jnp.concatenate(pieces + [filler], axis=0).T

    def body(i, _):
        r = i * chunk
        density = padded_ref[0, pl.ds(r, chunk + 4)]
        density = jnp.where(density == 0.0, 1.0, density)
        radial_speed = padded_ref[1, pl.ds(r, chunk + 4)] / density
        radial_weights = face_weights(radial_speed[1 : chunk + 2], radial_speed[2 : chunk + 3])
        speed = (padded_ref[2, pl.ds(r + 2, chunk)] / density[2 : 2 + chunk]).reshape(rows, width)
        weights = face_weights(speed, pltpu.roll(speed, width - 1, 1))
        side = sides[pl.ds(pl.multiple_of(r * layers, rows), rows)]
        for f in range(fields):
            values = padded_ref[f, pl.ds(r, chunk + 4)]
            centre = values[2 : 2 + chunk]
            first_step, first_flux, last_step, last_flux = [
                side[:, 4 * f + n : 4 * f + n + 1] for n in range(4)
            ]
            along = lane_divergence(
                centre.reshape(rows, width), weights, first_step, last_step, first_flux, last_flux
            ).reshape(chunk, layers, width)
            across = leading_divergence(values, radial_weights)
            next_ref[f, pl.ds(r, chunk)] = centre - radial_rate * across - azimuth_rate * along
        return 0

    lax.fori_loop(0, radii // chunk, body, 0)


def local(
    slabs,
    sectors,
    gas_fields,
    orbit_shift,
    particle_velocity,
    particle_mass,
    particle_stop,
    particle_cell,
    particle_dest,
):
    fields, radii, layers, sector = gas_fields.shape
    per_device = particle_dest.shape[0]
    devices = slabs * sectors
    capacity = 2 * per_device // devices
    own = radii // sectors
    rows = radii * layers
    slots = devices * capacity
    records = jnp.concatenate(
        [
            particle_velocity,
            particle_mass[None],
            particle_stop[None],
            particle_cell[None].astype(jnp.float32),
            jnp.zeros((2, per_device), jnp.float32),
        ],
        axis=0,
    )
    step = 512
    f32 = jnp.float32
    dma = pltpu.SemaphoreType.DMA
    padded, arrived_velocity, *edges = pl.pallas_call(
        functools.partial(step_kernel, slabs, sectors, step),
        out_shape=(
            jax.ShapeDtypeStruct((fields, radii + 4, layers, sector), f32),
            jax.ShapeDtypeStruct((3, slots), f32),
        )
        + (jax.ShapeDtypeStruct((fields, 8, rows), f32),) * 4,
        in_specs=[in_smem] + [in_vmem] * 3,
        out_specs=(in_vmem,) * 6,
        scratch_shapes=[pltpu.VMEM((sectors, own, layers, sector), f32)] * (2 * fields)
        + [
            pltpu.VMEM((devices, 8, capacity), f32),
            pltpu.VMEM((devices, 8, capacity), f32),
            pltpu.VMEM((3 * devices * 8, capacity), f32),
            pltpu.VMEM((3 * sector, 2 * rows), jnp.bfloat16),
            pltpu.VMEM((6 * sector, rows), f32),
        ]
        + [dma((fields, sectors))] * 4
        + [dma((devices,))] * 2
        + [dma((4,))] * 2,
        compiler_params=pltpu.CompilerParams(
            vmem_limit_bytes=VMEM_LIMIT, collective_id=0, has_side_effects=True
        ),
    )(orbit_shift, gas_fields, particle_dest.reshape(1, per_device), records)
    gas_next = pl.pallas_call(
        functools.partial(transport_kernel, 4),
        out_shape=jax.ShapeDtypeStruct(gas_fields.shape, f32),
        in_specs=[in_vmem] * 5,
        out_specs=in_vmem,
        scratch_shapes=[pltpu.VMEM((rows, 128), f32)],
        compiler_params=pltpu.CompilerParams(vmem_limit_bytes=VMEM_LIMIT),
    )(padded, *edges)
    return (gas_next, arrived_velocity)


def solution(mesh):
    placed = (
        P(None, "rad", None, "sec"),
        P("rad"),
        P(None, ("rad", "sec")),
        P(("rad", "sec")),
        P(("rad", "sec")),
        P(("rad", "sec")),
        P(("rad", "sec"), None),
    )
    return jax.shard_map(
        functools.partial(local, mesh.shape["rad"], mesh.shape["sec"]),
        mesh=mesh,
        in_specs=placed,
        out_specs=(P(None, "rad", None, "sec"), P(None, ("rad", "sec"))),
        check_vma=False,
    )
```
